512 devices in a mesh: occ: 128 (over y_lo, x, z, core), frag: 4 (over y_hi).
Axes of the slice: x: 4, y: 8 (y_hi: 4, y_lo: 2; y = y_hi * 2 + y_lo), z: 8, core: 2. Of those that a mesh axis runs over, the one named last changes fastest.
Arguments:
- factors: bfloat16 [512, 512, 1280], P(('frag', 'occ')), parts along dimension 0, may hold values from -1 to 1
- occ_energy: float32 [512], P('frag'), parts along dimension 0, may hold values from -2 to -0.3
- vir_energy: float32 [2048], P('frag'), parts along dimension 0, may hold values from 0.2 to 4
- coeffs: bfloat16 [4096, 512], P('frag'), parts along dimension 0, may hold values from -0.25 to 0.25
Outputs:
- back: bfloat16 [1280, 512, 1024], P('occ', 'frag'), parts along dimension 1
The draws below stay inside these ranges and needn't reach their ends.
There are 4 independent parts, one for each index of `frag`. The reference program is written for one: setup_inputs(seed, part) draws one part's arguments, and reference() takes and returns one part's arrays. A program takes and returns all parts, laid end to end along the dimension named above; each array names one. Nothing has to cross between parts.
All inputs are finite; a program needn't handle non-finite values.
Results may differ from the reference program's by a relative error of at most 0.008.
Values may be sent and summed in bfloat16 or wider, within the bound.
No kernel may reach another device: no remote copies, remote signals or barrier semaphores. Data moves between devices by JAX's collectives and lax.ppermute only.
A program may use at most 64 MiB of HBM per device.

```python
import jax
import jax.numpy as jnp
from jax import lax

V = 512
A = 1280
NAO = 1024
OFFSETS = 3
OCC = 128


def steps_of(own_key, extent, cuts, least, high):
    def one(position, shards_of):
        steps = jax.random.uniform(jax.random.fold_in(jax.random.fold_in(own_key, 6), position), (shards_of,), jnp.float32, least / len(cuts), high / len(cuts))
        return jnp.repeat(jnp.exp(steps), extent[position] // shards_of).reshape((-1,) + (1,) * (len(extent) - position - 1))

    loudness = one(*cuts[0])
    for cut in cuts[1:]:
        loudness = loudness * one(*cut)
    return loudness


def normal_values(own_key, extent, scale, bound, shards=(), held_as=jnp.bfloat16):
    gain = steps_of(own_key, extent, shards, -0.22, 0.18) if shards else 1.0
    array = jax.random.normal(own_key, extent, jnp.float32) * scale * gain
    return jnp.minimum(jnp.maximum(array, -bound), bound).astype(held_as)


def setup_inputs(seed: int = 0, part: int = 0) -> dict:
    seeds = jax.random.split(jax.random.key(seed), 5)
    own_keys = jax.random.split(jax.random.fold_in(seeds[4], part), 5)
    return {
        "factors": normal_values(own_keys[0], (OCC, V, A), 0.17, 1.0, ((0, 128),)),
        "occ_energy": jnp.clip(jax.random.uniform(own_keys[1], (OCC,), jnp.float32, -2.0, -0.3), -2.0, -0.3),
        "vir_energy": jnp.clip(jax.random.uniform(own_keys[2], (V,), jnp.float32, 0.2, 4.0), 0.2, 4.0),
        "coeffs": normal_values(own_keys[3], (NAO, V), V ** -0.5, 0.25),
    }


def rounded(value):
    return lax.optimization_barrier(value.astype(jnp.bfloat16)).astype(jnp.float32)


def reference(factors, occ_energy, vir_energy, coeffs):
    mine = factors.astype(jnp.float32)
    own = jnp.zeros((OCC, A, V), jnp.float32)
    incoming = jnp.zeros((OCC, A, V), jnp.float32)
    for offset in range(1, OFFSETS + 1):
        partner = jnp.roll(mine, -offset, axis=0)
        pair_energy = occ_energy + jnp.roll(occ_energy, -offset)
        kmat = jnp.einsum('iap,ibp->iab', mine, partner)
        denom = pair_energy[:, None, None] - vir_energy[None, :, None] - vir_energy[None, None, :]
        amps = rounded(kmat / denom)
        own = own + jnp.einsum('iab,ibp->ipa', amps, partner)
        sent = rounded(jnp.einsum('iap,iab->ipb', mine, amps))
        incoming = incoming + jnp.roll(sent, offset, axis=0)
    gamma = rounded(own + incoming)
    return jnp.einsum('ipa,ma->pim', gamma, coeffs.astype(jnp.float32)).astype(jnp.bfloat16)
```

```python
import jax
import jax.numpy as jnp
from jax import lax
from jax.sharding import Mesh
from jax.sharding import PartitionSpec as P

OCC = ("occ_0", "occ_1", "occ_2", "occ_3")
FRAG_OCC = ("frag",) + OCC


def mirrored(block, count, step):
    route = [(i, (i + step if i % 2 == 0 else i - step) % count) for i in range(count)]
    return lax.ppermute(block, OCC, route)


def on_device(factors, occ_energy, vir_energy, coeffs):
    mine = factors[0]
    virtuals, aux = mine.shape
    count = lax.axis_size(OCC)
    index = lax.axis_index(OCC)
    sign = 1 - 2 * (index % 2)
    plus2 = mirrored(mine, count, -2)
    minus2 = mirrored(mine, count, 2)
    plus1 = mirrored(mine, count, 1)
    minus3 = mirrored(plus2, count, -1)
    minus1 = mirrored(plus2, count, 1)
    plus3 = mirrored(minus2, count, 1)
    own_energy = lax.dynamic_index_in_dim(occ_energy, index, 0, False)

    def contribution(other, k):
        other_energy = lax.dynamic_index_in_dim(
            occ_energy, (index + sign * k) % count, 0, False
        )
        kmat = lax.dot_general(
            mine, other, (((1,), (1,)), ((), ())), preferred_element_type=jnp.float32
        )
        denom = own_energy + other_energy - vir_energy[:, None] - vir_energy[None, :]
        amps = (kmat / denom).astype(jnp.bfloat16)
        return lax.dot_general(
            amps, other, (((1,), (0,)), ((), ())), preferred_element_type=jnp.float32
        )

    total = contribution(plus1, 1)
    total = total + contribution(plus2, 2)
    total = total + contribution(minus2, -2)
    total = total + contribution(minus1, -1)
    total = total + contribution(plus3, 3)
    total = total + contribution(minus3, -3)
    gamma = total.T.astype(jnp.bfloat16)
    slabs = lax.all_to_all(gamma.reshape(count, -1, 128), OCC, 0, 0, tiled=True)
    slabs = slabs.reshape(count, aux // count, virtuals)
    return jnp.einsum("ipa,ma->pim", slabs, coeffs, preferred_element_type=jnp.float32).astype(
        jnp.bfloat16
    )


def solution(mesh):
    finer = Mesh(
        mesh.devices.reshape(2, 4, 8, 2, mesh.shape["frag"]),
        ("occ_0", "occ_1", "occ_2", "occ_3", "frag"),
    )
    in_specs = (P(FRAG_OCC, None, None), P("frag"), P("frag"), P("frag", None))
    out_specs = P(OCC, "frag", None)
    return jax.shard_map(
        on_device, mesh=finer, in_specs=in_specs, out_specs=out_specs, check_vma=False
    )
```

```python
import functools

import jax
import jax.numpy as jnp
from jax import lax
from jax.experimental import pallas as pl
from jax.experimental.pallas import tpu as pltpu
from jax.sharding import Mesh
from jax.sharding import PartitionSpec as P

OCC = ("occ_0", "occ_1", "occ_2", "occ_3")
FRAG_OCC = ("frag",) + OCC
LANES = 128
ROWS = 256
VMEM_LIMIT = 40 * 1024 * 1024

NT = (((1,), (1,)), ((), ()))
NN = (((1,), (0,)), ((), ()))


def mirrored(block, count, step):
    route = [(i, (i + step if i % 2 == 0 else i - step) % count) for i in range(count)]
    return lax.ppermute(block, OCC, route)


def pair_energy(steps, places, occ_energy):
    return occ_energy[places[steps[0] + 3]] + occ_energy[places[steps[1] + 3]]


def pair_term(steps, levels, part, left, right):
    places, occ_energy, column, row = levels
    energy = pair_energy(steps, places, occ_energy)
    kmat = lax.dot_general(left[part, :], right[...], NT, preferred_element_type=jnp.float32)
    amps = (kmat / (energy - column[part, :] - row[...])).astype(jnp.bfloat16)
    return lax.dot_general(amps, right[...], NN, preferred_element_type=jnp.float32)


def pairs_kernel(pairs, blocks, carried, again, *refs):
    levels, refs = refs[:4], refs[4:]
    held, refs = refs[:blocks], refs[blocks:]
    totals, outs = refs[:carried], refs[carried:]
    height = held[0].shape[0]
    for start in range(0, height, ROWS):
        part = pl.ds(start, ROWS)
        for k, (steps, left, right) in enumerate(pairs):
            value = pair_term(steps, levels, part, held[left], held[right])
            if k < carried:
                value = value + totals[k][part, :].astype(jnp.float32)
            outs[k][part, :] = value.astype(outs[k].dtype)
    if again:
        outs[-1][...] = held[0][...]


def pairs_sum(levels, blocks, pairs, totals=(), dtypes=(jnp.float32,), again=False):
    shape = blocks[0].shape
    vmem = pl.BlockSpec(memory_space=pltpu.VMEM)
    smem = pl.BlockSpec(memory_space=pltpu.SMEM)
    outs = [jax.ShapeDtypeStruct(shape, dtype) for dtype in dtypes]
    if again:
        outs.append(jax.ShapeDtypeStruct(shape, blocks[0].dtype))
    return pl.pallas_call(
        functools.partial(pairs_kernel, pairs, len(blocks), len(totals), again),
        out_shape=outs,
        in_specs=[smem] * 2 + [vmem] * (2 + len(blocks) + len(totals)),
        out_specs=[vmem] * len(outs),
        compiler_params=pltpu.CompilerParams(vmem_limit_bytes=VMEM_LIMIT),
        cost_estimate=pl.CostEstimate(flops=1000, bytes_accessed=1000, transcendentals=0),
        name="pairs",
    )(*levels, *blocks, *totals)


def last_kernel(steps, *refs):
    levels = refs[:4]
    mine, other, total, arrived, out, wide = refs[4:]
    virtuals, aux = mine.shape
    cols = virtuals // LANES
    for piece in range(cols):
        part = pl.ds(piece * LANES, LANES)
        value = pair_term(steps, levels, part, mine, other)
        value = value + total[part, :] + arrived[part, :].astype(jnp.float32)
        wide[pl.ds(piece, aux, stride=cols), :] = value.T
    out[...] = wide[...].astype(out.dtype)


def last_pair(levels, steps, mine, other, total, arrived):
    virtuals, aux = mine.shape
    cols = virtuals // LANES
    vmem = pl.BlockSpec(memory_space=pltpu.VMEM)
    smem = pl.BlockSpec(memory_space=pltpu.SMEM)
    return pl.pallas_call(
        functools.partial(last_kernel, steps),
        out_shape=jax.ShapeDtypeStruct((aux * cols, LANES), jnp.bfloat16),
        in_specs=[smem] * 2 + [vmem] * 6,
        out_specs=vmem,
        scratch_shapes=[pltpu.VMEM((aux * cols, LANES), jnp.float32)],
        compiler_params=pltpu.CompilerParams(vmem_limit_bytes=VMEM_LIMIT),
        cost_estimate=pl.CostEstimate(flops=1000, bytes_accessed=1000, transcendentals=0),
        name="last",
    )(*levels, mine, other, total, arrived)


def back_kernel(cols, chunk, slabs, coeffs, out, wide, flat):
    count = out.shape[1]
    height = slabs.shape[0] // count

    @pl.when(pl.program_id(0) == 0)
    def _():
        wide[...] = slabs[...].astype(jnp.float32)

    base = pl.program_id(0) * (chunk * cols)
    for p in range(chunk):
        for c in range(cols):
            piece = wide[pl.ds(base + p * cols + c, count, stride=height), :]
            flat[p * count : (p + 1) * count, c * LANES : (c + 1) * LANES] = piece.astype(
                jnp.bfloat16
            )
    back = lax.dot_general(flat[...], coeffs[...], NT, preferred_element_type=jnp.float32)
    out[...] = back.astype(out.dtype).reshape(out.shape)


def back_transform(slabs, coeffs, count):
    atoms, virtuals = coeffs.shape
    cols = virtuals // LANES
    rows = slabs.shape[0] // (count * cols)
    chunk = 2
    return pl.pallas_call(
        functools.partial(back_kernel, cols, chunk),
        grid=(rows // chunk,),
        out_shape=jax.ShapeDtypeStruct((rows, count, atoms), jnp.bfloat16),
        in_specs=[
            pl.BlockSpec(slabs.shape, lambda s: (0, 0)),
            pl.BlockSpec(coeffs.shape, lambda s: (0, 0)),
        ],
        out_specs=pl.BlockSpec((chunk, count, atoms), lambda s: (s, 0, 0)),
        scratch_shapes=[
            pltpu.VMEM(slabs.shape, jnp.float32),
            pltpu.VMEM((chunk * count, virtuals), jnp.bfloat16),
        ],
        compiler_params=pltpu.CompilerParams(vmem_limit_bytes=VMEM_LIMIT),
        cost_estimate=pl.CostEstimate(
            flops=2 * rows * count * virtuals * atoms,
            bytes_accessed=2 * rows * count * (virtuals + atoms),
            transcendentals=0,
        ),
        name="back",
    )(slabs, coeffs)


def on_device(factors, occ_energy, vir_energy, coeffs):
    mine = factors[0]
    count = lax.axis_size(OCC)
    index = lax.axis_index(OCC)
    sign = 1 - 2 * (index % 2)
    places = jnp.stack([(index + sign * k) % count for k in range(-3, 4)])
    levels = (places, occ_energy, vir_energy[:, None], vir_energy[None, :])
    f32, bf16 = jnp.float32, jnp.bfloat16

    plus2 = mirrored(mine, count, -2)
    plus1 = mirrored(mine, count, 1)
    total, again = pairs_sum(levels, [mine, plus1], [((0, 1), 0, 1)], again=True)
    minus2 = mirrored(again, count, 2)
    minus3 = mirrored(plus2, count, -1)
    total, beside = pairs_sum(
        levels, [mine, plus1, plus2], [((0, 2), 0, 2), ((1, 2), 1, 2)], [total], [f32, f32]
    )
    (beside,) = pairs_sum(levels, [plus1, minus2], [((1, -2), 0, 1)], [beside], [bf16])
    (total,) = pairs_sum(levels, [mine, minus2], [((0, -2), 0, 1)], [total])
    arrived = mirrored(beside, count, 1)
    gamma = last_pair(levels, (0, -3), mine, minus3, total, arrived)
    slabs = lax.all_to_all(gamma.reshape(count, -1, LANES), OCC, 0, 0, tiled=True)
    return back_transform(slabs.reshape(-1, LANES), coeffs, count)


def solution(mesh):
    finer = Mesh(
        mesh.devices.reshape(2, 4, 8, 2, mesh.shape["frag"]),
        ("occ_0", "occ_1", "occ_2", "occ_3", "frag"),
    )
    in_specs = (P(FRAG_OCC, None, None), P("frag"), P("frag"), P("frag", None))
    out_specs = P(OCC, "frag", None)
    return jax.shard_map(
        on_device, mesh=finer, in_specs=in_specs, out_specs=out_specs, check_vma=False
    )
```

```python
import functools

import jax
import jax.numpy as jnp
from jax import lax
from jax.experimental import pallas as pl
from jax.experimental.pallas import tpu as pltpu
from jax.sharding import Mesh
from jax.sharding import PartitionSpec as P

OCC = ("occ_0", "occ_1", "occ_2", "occ_3")
FRAG_OCC = ("frag",) + OCC
LANES = 128
PARTS = 2
VMEM_LIMIT = 40 * 1024 * 1024

NT = (((1,), (1,)), ((), ()))
TN = (((0,), (0,)), ((), ()))


def mirrored(block, count, step):
    route = [(i, (i + step if i % 2 == 0 else i - step) % count) for i in range(count)]
    return lax.ppermute(block, OCC, route)


def amplitudes(steps, levels, left, right):
    places, occ_energy, column, row = levels
    energy = occ_energy[places[steps[0] + 3]] + occ_energy[places[steps[1] + 3]]
    kmat = lax.dot_general(right[...], left[...], NT, preferred_element_type=jnp.float32)
    return (kmat / (energy - column[...] - row[...])).astype(jnp.bfloat16)


def pair_terms(amps, right):
    aux = right.shape[1]
    for start in range(0, aux, aux // PARTS):
        block = right[:, start : start + aux // PARTS]
        yield (
            pl.ds(start, aux // PARTS),
            lax.dot_general(block, amps, TN, preferred_element_type=jnp.float32),
        )


def pairs_kernel(pairs, blocks, carried, *refs):
    levels, refs = refs[:4], refs[4:]
    held, refs = refs[:blocks], refs[blocks:]
    totals, outs = refs[:carried], refs[carried:]
    for k, (steps, left, right) in enumerate(pairs):
        amps = amplitudes(steps, levels, held[left], held[right])
        for part, value in pair_terms(amps, held[right]):
            if k < carried:
                value = value + totals[k][part, :]
            outs[k][part, :] = value.astype(outs[k].dtype)


def first_kernel(steps, *refs):
    levels = refs[:4]
    mine, upper, lower, total, again, other = refs[4:]
    half = upper.shape[0]
    other[:half, :] = upper[...]
    other[half:, :] = lower[...]
    again[...] = mine[...]
    amps = amplitudes(steps, levels, mine, other)
    for part, value in pair_terms(amps, other):
        total[part, :] = value


def last_kernel(steps, *refs):
    levels = refs[:4]
    mine, other, total, arrived, out, wide = refs[4:]
    cols = mine.shape[0] // LANES
    amps = amplitudes(steps, levels, mine, other)
    for part, value in pair_terms(amps, other):
        value = value + total[part, :] + arrived[part, :].astype(jnp.float32)
        for c in range(cols):
            rows = pl.ds(part.start * cols + c, part.size, stride=cols)
            wide[rows, :] = value[:, c * LANES : (c + 1) * LANES]
    out[...] = wide[...].astype(out.dtype)


def local_call(kernel, levels, arrays, outs, scratch=(), name=None, flops=1000):
    vmem = pl.BlockSpec(memory_space=pltpu.VMEM)
    smem = pl.BlockSpec(memory_space=pltpu.SMEM)
    return pl.pallas_call(
        kernel,
        out_shape=[jax.ShapeDtypeStruct(shape, dtype) for shape, dtype in outs],
        in_specs=[smem] * 2 + [vmem] * (2 + len(arrays)),
        out_specs=[vmem] * len(outs),
        scratch_shapes=list(scratch),
        compiler_params=pltpu.CompilerParams(vmem_limit_bytes=VMEM_LIMIT),
        cost_estimate=pl.CostEstimate(flops=flops, bytes_accessed=1000, transcendentals=0),
        name=name,
    )(*levels, *arrays)


def pairs_sum(levels, blocks, pairs, totals, dtypes):
    shape = blocks[0].shape[::-1]
    kernel = functools.partial(pairs_kernel, pairs, len(blocks), len(totals))
    outs = [(shape, dtype) for dtype in dtypes]
    flops = 10**10 if len(pairs) > 1 else 1000
    return local_call(kernel, levels, [*blocks, *totals], outs, name="pairs", flops=flops)


def first_pair(levels, steps, mine, upper, lower):
    block = (mine.shape, mine.dtype)
    outs = [(mine.shape[::-1], jnp.float32), block, block]
    kernel = functools.partial(first_kernel, steps)
    return local_call(kernel, levels, [mine, upper, lower], outs, name="first")


def last_pair(levels, steps, mine, other, total, arrived):
    shape = (mine.size // LANES, LANES)
    kernel = functools.partial(last_kernel, steps)
    (gamma,) = local_call(
        kernel,
        levels,
        [mine, other, total, arrived],
        [(shape, jnp.bfloat16)],
        [pltpu.VMEM(shape, jnp.float32)],
        name="last",
    )
    return gamma


def back_kernel(chunk, slabs, coeffs, out, wide, flat, done, sems):
    rows, count, _ = done.shape
    cols = coeffs.shape[1] // LANES
    wide[...] = slabs[...].astype(jnp.float32)
    copies = []
    for k in range(rows // chunk):
        for p in range(chunk):
            for c in range(cols):
                source = pl.ds(((k * chunk + p) * cols) + c, count, stride=rows * cols)
                flat[p * count : (p + 1) * count, c * LANES : (c + 1) * LANES] = wide[
                    source, :
                ].astype(flat.dtype)
        back = lax.dot_general(flat[...], coeffs[...], NT, preferred_element_type=jnp.float32)
        part = pl.ds(k * chunk, chunk)
        done[part] = back.astype(done.dtype).reshape(chunk, count, -1)
        copies.append(pltpu.make_async_copy(done.at[part], out.at[part], sems.at[k]))
        copies[-1].start()
    for copy in copies:
        copy.wait()


def back_transform(slabs, coeffs, count):
    atoms, virtuals = coeffs.shape
    rows = slabs.size // (count * virtuals)
    chunk = 2
    shape = (rows, count, atoms)
    vmem = pl.BlockSpec(memory_space=pltpu.VMEM)
    return pl.pallas_call(
        functools.partial(back_kernel, chunk),
        out_shape=jax.ShapeDtypeStruct(shape, jnp.bfloat16),
        in_specs=[vmem, vmem],
        out_specs=pl.BlockSpec(memory_space=pl.ANY),
        scratch_shapes=[
            pltpu.VMEM(slabs.shape, jnp.float32),
            pltpu.VMEM((chunk * count, virtuals), jnp.bfloat16),
            pltpu.VMEM(shape, jnp.bfloat16),
            pltpu.SemaphoreType.DMA((rows // chunk,)),
        ],
        compiler_params=pltpu.CompilerParams(vmem_limit_bytes=VMEM_LIMIT),
        cost_estimate=pl.CostEstimate(
            flops=2 * rows * count * virtuals * atoms,
            bytes_accessed=2 * rows * count * (virtuals + atoms),
            transcendentals=0,
        ),
        name="back",
    )(slabs, coeffs)


def on_device(factors, occ_energy, vir_energy, coeffs):
    mine = factors[0]
    count = lax.axis_size(OCC)
    index = lax.axis_index(OCC)
    sign = 1 - 2 * (index % 2)
    places = jnp.stack([(index + sign * k) % count for k in range(-3, 4)])
    levels = (places, occ_energy, vir_energy[:, None], vir_energy[None, :])
    f32, bf16 = jnp.float32, jnp.bfloat16

    half = mine.shape[0] // 2
    plus2 = mirrored(mine, count, -2)
    upper = mirrored(mine[:half], count, 1)
    lower = mirrored(mine[half:], count, 1)
    total, again, plus1 = first_pair(levels, (0, 1), mine, upper, lower)
    minus2 = mirrored(again, count, 2)
    minus3 = mirrored(plus2, count, -1)
    total, beside = pairs_sum(
        levels, [mine, plus1, plus2], [((0, 2), 0, 2), ((1, 2), 1, 2)], [total], [f32, f32]
    )
    (beside,) = pairs_sum(levels, [plus1, minus2], [((1, -2), 0, 1)], [beside], [bf16])
    (total,) = pairs_sum(levels, [mine, minus2], [((0, -2), 0, 1)], [total], [f32])
    arrived = mirrored(beside, count, 1)
    gamma = last_pair(levels, (0, -3), mine, minus3, total, arrived)
    slabs = lax.all_to_all(gamma.reshape(count, -1, LANES), OCC, 0, 0, tiled=True)
    return back_transform(slabs.reshape(-1, LANES), coeffs, count)


def solution(mesh):
    finer = Mesh(
        mesh.devices.reshape(2, 4, 8, 2, mesh.shape["frag"]),
        ("occ_0", "occ_1", "occ_2", "occ_3", "frag"),
    )
    in_specs = (P(FRAG_OCC, None, None), P("frag"), P("frag"), P("frag", None))
    out_specs = P(OCC, "frag", None)
    return jax.shard_map(
        on_device, mesh=finer, in_specs=in_specs, out_specs=out_specs, check_vma=False
    )
```

```python
import functools

import jax
import jax.numpy as jnp
from jax import lax
from jax.experimental import pallas as pl
from jax.experimental.pallas import tpu as pltpu
from jax.sharding import Mesh
from jax.sharding import PartitionSpec as P

OCC = ("occ_0", "occ_1", "occ_2", "occ_3")
FRAG_OCC = ("frag",) + OCC
LANES = 128
PARTS = 2
VMEM_LIMIT = 40 * 1024 * 1024

NT = (((1,), (1,)), ((), ()))
TN = (((0,), (0,)), ((), ()))


def mirrored(block, count, step):
    route = [(i, (i + step if i % 2 == 0 else i - step) % count) for i in range(count)]
    return lax.ppermute(block, OCC, route)


def amplitudes(steps, levels, left, right):
    places, occ_energy, column, row = levels
    energy = occ_energy[places[steps[0] + 3]] + occ_energy[places[steps[1] + 3]]
    kmat = lax.dot_general(right[...], left[...], NT, preferred_element_type=jnp.float32)
    return (kmat / (energy - column[...] - row[...])).astype(jnp.bfloat16)


def pair_terms(amps, right):
    aux = right.shape[1]
    for start in range(0, aux, aux // PARTS):
        block = right[:, start : start + aux // PARTS]
        yield (
            pl.ds(start, aux // PARTS),
            lax.dot_general(block, amps, TN, preferred_element_type=jnp.float32),
        )


def pairs_kernel(pairs, blocks, carried, pieces, *refs):
    levels, refs = refs[:4], refs[4:]
    held, refs = refs[:blocks], refs[blocks:]
    totals, outs = refs[:carried], refs[carried:]
    for k, (steps, left, right) in enumerate(pairs):
        amps = amplitudes(steps, levels, held[left], held[right])
        for n, (part, value) in enumerate(pair_terms(amps, held[right])):
            if k < carried:
                value = value + totals[k][part, :]
            if pieces:
                outs[n][...] = value.astype(outs[n].dtype)
            else:
                outs[k][part, :] = value


def first_kernel(steps, *refs):
    levels = refs[:4]
    mine, upper, lower, total, other = refs[4:]
    half = upper.shape[0]
    other[:half, :] = upper[...]
    other[half:, :] = lower[...]
    amps = amplitudes(steps, levels, mine, other)
    for part, value in pair_terms(amps, other):
        total[part, :] = value


def split_kernel(mine, upper, lower, again):
    half = upper.shape[0]
    upper[...] = mine[:half, :]
    lower[...] = mine[half:, :]
    again[...] = mine[...]


def split(mine):
    rows, aux = mine.shape
    vmem = pl.BlockSpec(memory_space=pltpu.VMEM)
    return pl.pallas_call(
        split_kernel,
        out_shape=[
            jax.ShapeDtypeStruct((height, aux), mine.dtype)
            for height in (rows // 2, rows // 2, rows)
        ],
        in_specs=[vmem],
        out_specs=[vmem] * 3,
        compiler_params=pltpu.CompilerParams(vmem_limit_bytes=VMEM_LIMIT),
        cost_estimate=pl.CostEstimate(flops=1000, bytes_accessed=1000, transcendentals=0),
        name="split",
    )(mine)


def last_kernel(steps, *refs):
    levels = refs[:4]
    mine, other, total, *arrived, out, wide = refs[4:]
    cols = mine.shape[0] // LANES
    amps = amplitudes(steps, levels, mine, other)
    for piece, (part, value) in zip(arrived, pair_terms(amps, other)):
        value = value + total[part, :] + piece[...].astype(jnp.float32)
        for c in range(cols):
            rows = pl.ds(part.start * cols + c, part.size, stride=cols)
            wide[rows, :] = value[:, c * LANES : (c + 1) * LANES]
    out[...] = wide[...].astype(out.dtype)


def local_call(kernel, levels, arrays, outs, scratch=(), name=None, flops=1000):
    vmem = pl.BlockSpec(memory_space=pltpu.VMEM)
    smem = pl.BlockSpec(memory_space=pltpu.SMEM)
    return pl.pallas_call(
        kernel,
        out_shape=[jax.ShapeDtypeStruct(shape, dtype) for shape, dtype in outs],
        in_specs=[smem] * 2 + [vmem] * (2 + len(arrays)),
        out_specs=[vmem] * len(outs),
        scratch_shapes=list(scratch),
        compiler_params=pltpu.CompilerParams(vmem_limit_bytes=VMEM_LIMIT),
        cost_estimate=pl.CostEstimate(flops=flops, bytes_accessed=1000, transcendentals=0),
        name=name,
    )(*levels, *arrays)


def pairs_sum(levels, blocks, pairs, totals, pieces=0):
    virtuals, aux = blocks[0].shape
    kernel = functools.partial(pairs_kernel, pairs, len(blocks), len(totals), pieces)
    outs = [((aux, virtuals), jnp.float32)] * len(pairs)
    if pieces:
        outs = [((aux // pieces, virtuals), jnp.bfloat16)] * pieces
    flops = 10**10 if len(pairs) > 1 else 1000
    return local_call(kernel, levels, [*blocks, *totals], outs, name="pairs", flops=flops)


def first_pair(levels, steps, mine, upper, lower):
    outs = [(mine.shape[::-1], jnp.float32), (mine.shape, mine.dtype)]
    kernel = functools.partial(first_kernel, steps)
    return local_call(kernel, levels, [mine, upper, lower], outs, name="first")


def last_pair(levels, steps, mine, other, total, arrived):
    shape = (mine.size // LANES, LANES)
    kernel = functools.partial(last_kernel, steps)
    (gamma,) = local_call(
        kernel,
        levels,
        [mine, other, total, *arrived],
        [(shape, jnp.bfloat16)],
        [pltpu.VMEM(shape, jnp.float32)],
        name="last",
    )
    return gamma


def back_kernel(chunk, slabs, coeffs, out, wide, flat, done, sems):
    rows, count, _ = done.shape
    cols = coeffs.shape[1] // LANES
    wide[...] = slabs[...].astype(jnp.float32)
    copies = []
    for k in range(rows // chunk):
        for p in range(chunk):
            for c in range(cols):
                source = pl.ds(((k * chunk + p) * cols) + c, count, stride=rows * cols)
                flat[p * count : (p + 1) * count, c * LANES : (c + 1) * LANES] = wide[
                    source, :
                ].astype(flat.dtype)
        back = lax.dot_general(flat[...], coeffs[...], NT, preferred_element_type=jnp.float32)
        part = pl.ds(k * chunk, chunk)
        done[part] = back.astype(done.dtype).reshape(chunk, count, -1)
        copies.append(pltpu.make_async_copy(done.at[part], out.at[part], sems.at[k]))
        copies[-1].start()
    for copy in copies:
        copy.wait()


def back_transform(slabs, coeffs, count):
    atoms, virtuals = coeffs.shape
    rows = slabs.size // (count * virtuals)
    chunk = 2
    shape = (rows, count, atoms)
    vmem = pl.BlockSpec(memory_space=pltpu.VMEM)
    return pl.pallas_call(
        functools.partial(back_kernel, chunk),
        out_shape=jax.ShapeDtypeStruct(shape, jnp.bfloat16),
        in_specs=[vmem, vmem],
        out_specs=pl.BlockSpec(memory_space=pl.ANY),
        scratch_shapes=[
            pltpu.VMEM(slabs.shape, jnp.float32),
            pltpu.VMEM((chunk * count, virtuals), jnp.bfloat16),
            pltpu.VMEM(shape, jnp.bfloat16),
            pltpu.SemaphoreType.DMA((rows // chunk,)),
        ],
        compiler_params=pltpu.CompilerParams(vmem_limit_bytes=VMEM_LIMIT),
        cost_estimate=pl.CostEstimate(
            flops=2 * rows * count * virtuals * atoms,
            bytes_accessed=2 * rows * count * (virtuals + atoms),
            transcendentals=0,
        ),
        name="back",
    )(slabs, coeffs)


def on_device(factors, occ_energy, vir_energy, coeffs):
    mine = factors[0]
    count = lax.axis_size(OCC)
    index = lax.axis_index(OCC)
    sign = 1 - 2 * (index % 2)
    places = jnp.stack([(index + sign * k) % count for k in range(-3, 4)])
    levels = (places, occ_energy, vir_energy[:, None], vir_energy[None, :])

    plus2 = mirrored(mine, count, -2)
    upper, lower, again = split(mine)
    minus2 = mirrored(again, count, 2)
    upper, lower = mirrored(upper, count, 1), mirrored(lower, count, 1)
    total, plus1 = first_pair(levels, (0, 1), mine, upper, lower)
    minus3 = mirrored(plus2, count, -1)
    total, beside = pairs_sum(
        levels, [mine, plus1, plus2], [((0, 2), 0, 2), ((1, 2), 1, 2)], [total]
    )
    beside = pairs_sum(levels, [plus1, minus2], [((1, -2), 0, 1)], [beside], PARTS)
    (total,) = pairs_sum(levels, [mine, minus2], [((0, -2), 0, 1)], [total])
    arrived = [mirrored(piece, count, 1) for piece in beside]
    gamma = last_pair(levels, (0, -3), mine, minus3, total, arrived)
    slabs = lax.all_to_all(gamma.reshape(count, -1, LANES), OCC, 0, 0, tiled=True)
    return back_transform(slabs.reshape(-1, LANES), coeffs, count)


def solution(mesh):
    finer = Mesh(
        mesh.devices.reshape(2, 4, 8, 2, mesh.shape["frag"]),
        ("occ_0", "occ_1", "occ_2", "occ_3", "frag"),
    )
    in_specs = (P(FRAG_OCC, None, None), P("frag"), P("frag"), P("frag", None))
    out_specs = P(OCC, "frag", None)
    return jax.shard_map(
        on_device, mesh=finer, in_specs=in_specs, out_specs=out_specs, check_vma=False
    )
```

```python
import functools

import jax
import jax.numpy as jnp
from jax import lax
from jax.experimental import pallas as pl
from jax.experimental.pallas import tpu as pltpu
from jax.sharding import Mesh
from jax.sharding import PartitionSpec as P

OCC = ("occ_0", "occ_1", "occ_2", "occ_3")
FRAG_OCC = ("frag",) + OCC
LANES = 128
PARTS = 2
VMEM_LIMIT = 40 * 1024 * 1024

NT = (((1,), (1,)), ((), ()))
TN = (((0,), (0,)), ((), ()))


def mirrored(block, count, step):
    route = [(i, (i + step if i % 2 == 0 else i - step) % count) for i in range(count)]
    return lax.ppermute(block, OCC, route)


def amplitudes(steps, levels, left, right):
    places, occ_energy, column, row = levels
    energy = occ_energy[places[steps[0] + 3]] + occ_energy[places[steps[1] + 3]]
    kmat = lax.dot_general(right[...], left[...], NT, preferred_element_type=jnp.float32)
    return (kmat / (energy - column[...] - row[...])).astype(jnp.bfloat16)


def pair_terms(amps, right):
    aux = right.shape[1]
    for start in range(0, aux, aux // PARTS):
        block = right[:, start : start + aux // PARTS]
        yield (
            pl.ds(start, aux // PARTS),
            lax.dot_general(block, amps, TN, preferred_element_type=jnp.float32),
        )


def pairs_kernel(pairs, blocks, carried, *refs):
    levels, refs = refs[:4], refs[4:]
    held, refs = refs[:blocks], refs[blocks:]
    totals, outs = refs[:carried], refs[carried:]
    for k, (steps, left, right) in enumerate(pairs):
        amps = amplitudes(steps, levels, held[left], held[right])
        for part, value in pair_terms(amps, held[right]):
            if k < carried:
                value = value + totals[k][part, :]
            outs[k][part, :] = value.astype(outs[k].dtype)


def first_kernel(steps, *refs):
    levels = refs[:4]
    mine, upper, lower, total, other = refs[4:]
    half = upper.shape[0]
    other[:half, :] = upper[...]
    other[half:, :] = lower[...]
    amps = amplitudes(steps, levels, mine, other)
    for part, value in pair_terms(amps, other):
        total[part, :] = value


def split_kernel(mine, upper, lower, again):
    half = upper.shape[0]
    upper[...] = mine[:half, :]
    lower[...] = mine[half:, :]
    again[...] = mine[...]


def split(mine):
    rows, aux = mine.shape
    vmem = pl.BlockSpec(memory_space=pltpu.VMEM)
    return pl.pallas_call(
        split_kernel,
        out_shape=[
            jax.ShapeDtypeStruct((height, aux), mine.dtype)
            for height in (rows // 2, rows // 2, rows)
        ],
        in_specs=[vmem],
        out_specs=[vmem] * 3,
        compiler_params=pltpu.CompilerParams(vmem_limit_bytes=VMEM_LIMIT),
        cost_estimate=pl.CostEstimate(flops=1000, bytes_accessed=1000, transcendentals=0),
        name="split",
    )(mine)


def amps_kernel(steps, *refs):
    levels = refs[:4]
    mine, other, out = refs[4:]
    out[...] = amplitudes(steps, levels, mine, other)


def last_kernel(amps, other, total, arrived, out, wide):
    cols = other.shape[0] // LANES
    for part, value in pair_terms(amps[...], other):
        value = value + total[part, :] + arrived[part, :].astype(jnp.float32)
        for c in range(cols):
            rows = pl.ds(part.start * cols + c, part.size, stride=cols)
            wide[rows, :] = value[:, c * LANES : (c + 1) * LANES]
    out[...] = wide[...].astype(out.dtype)


def local_call(kernel, levels, arrays, outs, scratch=(), name=None, flops=1000):
    vmem = pl.BlockSpec(memory_space=pltpu.VMEM)
    smem = pl.BlockSpec(memory_space=pltpu.SMEM)
    return pl.pallas_call(
        kernel,
        out_shape=[jax.ShapeDtypeStruct(shape, dtype) for shape, dtype in outs],
        in_specs=[smem] * 2 + [vmem] * (2 + len(arrays)),
        out_specs=[vmem] * len(outs),
        scratch_shapes=list(scratch),
        compiler_params=pltpu.CompilerParams(vmem_limit_bytes=VMEM_LIMIT),
        cost_estimate=pl.CostEstimate(flops=flops, bytes_accessed=1000, transcendentals=0),
        name=name,
    )(*levels, *arrays)


def pairs_sum(levels, blocks, pairs, totals, dtypes):
    shape = blocks[0].shape[::-1]
    kernel = functools.partial(pairs_kernel, pairs, len(blocks), len(totals))
    outs = [(shape, dtype) for dtype in dtypes]
    flops = 10**10 if len(pairs) > 1 else 1000
    return local_call(kernel, levels, [*blocks, *totals], outs, name="pairs", flops=flops)


def first_pair(levels, steps, mine, upper, lower):
    outs = [(mine.shape[::-1], jnp.float32), (mine.shape, mine.dtype)]
    kernel = functools.partial(first_kernel, steps)
    return local_call(kernel, levels, [mine, upper, lower], outs, name="first")


def last_pair(levels, steps, mine, other, total, arrived):
    virtuals, aux = mine.shape
    kernel = functools.partial(amps_kernel, steps)
    outs = [((virtuals, virtuals), jnp.bfloat16)]
    (amps,) = local_call(kernel, levels, [mine, other], outs, name="amps")
    shape = (mine.size // LANES, LANES)
    vmem = pl.BlockSpec(memory_space=pltpu.VMEM)
    return pl.pallas_call(
        last_kernel,
        out_shape=jax.ShapeDtypeStruct(shape, jnp.bfloat16),
        in_specs=[vmem] * 4,
        out_specs=vmem,
        scratch_shapes=[pltpu.VMEM(shape, jnp.float32)],
        compiler_params=pltpu.CompilerParams(vmem_limit_bytes=VMEM_LIMIT),
        cost_estimate=pl.CostEstimate(flops=1000, bytes_accessed=1000, transcendentals=0),
        name="last",
    )(amps, other, total, arrived)


def back_kernel(chunk, slabs, coeffs, out, wide, flat, done, sems):
    rows, count, _ = done.shape
    cols = coeffs.shape[1] // LANES
    wide[...] = slabs[...].astype(jnp.float32)
    copies = []
    for k in range(rows // chunk):
        for p in range(chunk):
            for c in range(cols):
                source = pl.ds(((k * chunk + p) * cols) + c, count, stride=rows * cols)
                flat[p * count : (p + 1) * count, c * LANES : (c + 1) * LANES] = wide[
                    source, :
                ].astype(flat.dtype)
        back = lax.dot_general(flat[...], coeffs[...], NT, preferred_element_type=jnp.float32)
        part = pl.ds(k * chunk, chunk)
        done[part] = back.astype(done.dtype).reshape(chunk, count, -1)
        copies.append(pltpu.make_async_copy(done.at[part], out.at[part], sems.at[k]))
        copies[-1].start()
    for copy in copies:
        copy.wait()


def back_transform(slabs, coeffs, count):
    atoms, virtuals = coeffs.shape
    rows = slabs.size // (count * virtuals)
    chunk = 2
    shape = (rows, count, atoms)
    vmem = pl.BlockSpec(memory_space=pltpu.VMEM)
    return pl.pallas_call(
        functools.partial(back_kernel, chunk),
        out_shape=jax.ShapeDtypeStruct(shape, jnp.bfloat16),
        in_specs=[vmem, vmem],
        out_specs=pl.BlockSpec(memory_space=pl.ANY),
        scratch_shapes=[
            pltpu.VMEM(slabs.shape, jnp.float32),
            pltpu.VMEM((chunk * count, virtuals), jnp.bfloat16),
            pltpu.VMEM(shape, jnp.bfloat16),
            pltpu.SemaphoreType.DMA((rows // chunk,)),
        ],
        compiler_params=pltpu.CompilerParams(vmem_limit_bytes=VMEM_LIMIT),
        cost_estimate=pl.CostEstimate(
            flops=2 * rows * count * virtuals * atoms,
            bytes_accessed=2 * rows * count * (virtuals + atoms),
            transcendentals=0,
        ),
        name="back",
    )(slabs, coeffs)


def on_device(factors, occ_energy, vir_energy, coeffs):
    mine = factors[0]
    count = lax.axis_size(OCC)
    index = lax.axis_index(OCC)
    sign = 1 - 2 * (index % 2)
    places = jnp.stack([(index + sign * k) % count for k in range(-3, 4)])
    levels = (places, occ_energy, vir_energy[:, None], vir_energy[None, :])
    f32, bf16 = jnp.float32, jnp.bfloat16

    plus2 = mirrored(mine, count, -2)
    upper, lower, again = split(mine)
    minus2 = mirrored(again, count, 2)
    upper, lower = mirrored(upper, count, 1), mirrored(lower, count, 1)
    total, plus1 = first_pair(levels, (0, 1), mine, upper, lower)
    minus3 = mirrored(plus2, count, -1)
    total, beside = pairs_sum(
        levels, [mine, plus1, plus2], [((0, 2), 0, 2), ((1, 2), 1, 2)], [total], [f32, f32]
    )
    (beside,) = pairs_sum(levels, [plus1, minus2], [((1, -2), 0, 1)], [beside], [bf16])
    (total,) = pairs_sum(levels, [mine, minus2], [((0, -2), 0, 1)], [total], [f32])
    arrived = mirrored(beside, count, 1)
    gamma = last_pair(levels, (0, -3), mine, minus3, total, arrived)
    slabs = lax.all_to_all(gamma.reshape(count, -1, LANES), OCC, 0, 0, tiled=True)
    return back_transform(slabs.reshape(-1, LANES), coeffs, count)


def solution(mesh):
    finer = Mesh(
        mesh.devices.reshape(2, 4, 8, 2, mesh.shape["frag"]),
        ("occ_0", "occ_1", "occ_2", "occ_3", "frag"),
    )
    in_specs = (P(FRAG_OCC, None, None), P("frag"), P("frag"), P("frag", None))
    out_specs = P(OCC, "frag", None)
    return jax.shard_map(
        on_device, mesh=finer, in_specs=in_specs, out_specs=out_specs, check_vma=False
    )
```

```python
import functools

import jax
import jax.numpy as jnp
from jax import lax
from jax.experimental import pallas as pl
from jax.experimental.pallas import tpu as pltpu
from jax.sharding import Mesh
from jax.sharding import PartitionSpec as P

OCC = ("occ_0", "occ_1", "occ_2", "occ_3")
FRAG_OCC = ("frag",) + OCC
LANES = 128
PARTS = 2
VMEM_LIMIT = 40 * 1024 * 1024

NT = (((1,), (1,)), ((), ()))
TN = (((0,), (0,)), ((), ()))


def mirrored(block, count, step):
    route = [(i, (i + step if i % 2 == 0 else i - step) % count) for i in range(count)]
    return lax.ppermute(block, OCC, route)


def amplitudes(steps, levels, left, right):
    places, occ_energy, column, row = levels
    energy = occ_energy[places[steps[0] + 3]] + occ_energy[places[steps[1] + 3]]
    kmat = lax.dot_general(right[...], left[...], NT, preferred_element_type=jnp.float32)
    return (kmat / (energy - column[...] - row[...])).astype(jnp.bfloat16)


def pair_terms(amps, right):
    aux = right.shape[1]
    for start in range(0, aux, aux // PARTS):
        block = right[:, start : start + aux // PARTS]
        yield (
            pl.ds(start, aux // PARTS),
            lax.dot_general(block, amps, TN, preferred_element_type=jnp.float32),
        )


def pairs_kernel(pairs, blocks, carried, *refs):
    levels, refs = refs[:4], refs[4:]
    held, refs = refs[:blocks], refs[blocks:]
    totals, outs = refs[:carried], refs[carried:]
    for k, (steps, left, right) in enumerate(pairs):
        amps = amplitudes(steps, levels, held[left], held[right])
        for part, value in pair_terms(amps, held[right]):
            if k < carried:
                value = value + totals[k][part, :]
            outs[k][part, :] = value.astype(outs[k].dtype)


def first_kernel(steps, *refs):
    levels = refs[:4]
    mine, upper, lower, total, other = refs[4:]
    half = upper.shape[0]
    other[:half, :] = upper[...]
    other[half:, :] = lower[...]
    amps = amplitudes(steps, levels, mine, other)
    for part, value in pair_terms(amps, other):
        total[part, :] = value


def split_kernel(mine, upper, lower, again):
    half = upper.shape[0]
    upper[...] = mine[:half, :]
    lower[...] = mine[half:, :]
    again[...] = mine[...]


def split(mine):
    rows, aux = mine.shape
    vmem = pl.BlockSpec(memory_space=pltpu.VMEM)
    return pl.pallas_call(
        split_kernel,
        out_shape=[
            jax.ShapeDtypeStruct((height, aux), mine.dtype)
            for height in (rows // 2, rows // 2, rows)
        ],
        in_specs=[vmem],
        out_specs=[vmem] * 3,
        compiler_params=pltpu.CompilerParams(vmem_limit_bytes=VMEM_LIMIT),
        cost_estimate=pl.CostEstimate(flops=1000, bytes_accessed=1000, transcendentals=0),
        name="split",
    )(mine)


def amps_kernel(steps, *refs):
    levels = refs[:4]
    mine, other, out = refs[4:]
    out[...] = amplitudes(steps, levels, mine, other)


def last_kernel(amps, other, total, arrived, out, wide):
    cols = other.shape[0] // LANES
    for part, value in pair_terms(amps[...], other):
        value = value + total[part, :] + arrived[part, :].astype(jnp.float32)
        for c in range(cols):
            rows = pl.ds(part.start * cols + c, part.size, stride=cols)
            wide[rows, :] = value[:, c * LANES : (c + 1) * LANES]
    out[...] = wide[...].astype(out.dtype)


def local_call(kernel, levels, arrays, outs, scratch=(), name=None):
    vmem = pl.BlockSpec(memory_space=pltpu.VMEM)
    smem = pl.BlockSpec(memory_space=pltpu.SMEM)
    return pl.pallas_call(
        kernel,
        out_shape=[jax.ShapeDtypeStruct(shape, dtype) for shape, dtype in outs],
        in_specs=[smem] * 2 + [vmem] * (2 + len(arrays)),
        out_specs=[vmem] * len(outs),
        scratch_shapes=list(scratch),
        compiler_params=pltpu.CompilerParams(vmem_limit_bytes=VMEM_LIMIT),
        cost_estimate=pl.CostEstimate(flops=1000, bytes_accessed=1000, transcendentals=0),
        name=name,
    )(*levels, *arrays)


def pairs_sum(levels, blocks, pairs, totals, dtypes):
    shape = blocks[0].shape[::-1]
    kernel = functools.partial(pairs_kernel, pairs, len(blocks), len(totals))
    outs = [(shape, dtype) for dtype in dtypes]
    return local_call(kernel, levels, [*blocks, *totals], outs, name="pairs")


def first_pair(levels, steps, mine, upper, lower):
    outs = [(mine.shape[::-1], jnp.float32), (mine.shape, mine.dtype)]
    kernel = functools.partial(first_kernel, steps)
    return local_call(kernel, levels, [mine, upper, lower], outs, name="first")


def last_pair(levels, steps, mine, other, total, arrived):
    virtuals, aux = mine.shape
    kernel = functools.partial(amps_kernel, steps)
    outs = [((virtuals, virtuals), jnp.bfloat16)]
    (amps,) = local_call(kernel, levels, [mine, other], outs, name="amps")
    shape = (mine.size // LANES, LANES)
    vmem = pl.BlockSpec(memory_space=pltpu.VMEM)
    return pl.pallas_call(
        last_kernel,
        out_shape=jax.ShapeDtypeStruct(shape, jnp.bfloat16),
        in_specs=[vmem] * 4,
        out_specs=vmem,
        scratch_shapes=[pltpu.VMEM(shape, jnp.float32)],
        compiler_params=pltpu.CompilerParams(vmem_limit_bytes=VMEM_LIMIT),
        cost_estimate=pl.CostEstimate(flops=1000, bytes_accessed=1000, transcendentals=0),
        name="last",
    )(amps, other, total, arrived)


def back_kernel(chunk, slabs, coeffs, out, wide, flat, done, sems):
    rows, count, _ = done.shape
    cols = coeffs.shape[1] // LANES
    wide[...] = slabs[...].astype(jnp.float32)
    copies = []
    for k in range(rows // chunk):
        for p in range(chunk):
            for c in range(cols):
                source = pl.ds(((k * chunk + p) * cols) + c, count, stride=rows * cols)
                flat[p * count : (p + 1) * count, c * LANES : (c + 1) * LANES] = wide[
                    source, :
                ].astype(flat.dtype)
        back = lax.dot_general(flat[...], coeffs[...], NT, preferred_element_type=jnp.float32)
        part = pl.ds(k * chunk, chunk)
        done[part] = back.astype(done.dtype).reshape(chunk, count, -1)
        copies.append(pltpu.make_async_copy(done.at[part], out.at[part], sems.at[k]))
        copies[-1].start()
    for copy in copies:
        copy.wait()


def back_transform(slabs, coeffs, count):
    atoms, virtuals = coeffs.shape
    rows = slabs.size // (count * virtuals)
    chunk = 2
    shape = (rows, count, atoms)
    vmem = pl.BlockSpec(memory_space=pltpu.VMEM)
    return pl.pallas_call(
        functools.partial(back_kernel, chunk),
        out_shape=jax.ShapeDtypeStruct(shape, jnp.bfloat16),
        in_specs=[vmem, vmem],
        out_specs=pl.BlockSpec(memory_space=pl.ANY),
        scratch_shapes=[
            pltpu.VMEM(slabs.shape, jnp.float32),
            pltpu.VMEM((chunk * count, virtuals), jnp.bfloat16),
            pltpu.VMEM(shape, jnp.bfloat16),
            pltpu.SemaphoreType.DMA((rows // chunk,)),
        ],
        compiler_params=pltpu.CompilerParams(vmem_limit_bytes=VMEM_LIMIT),
        cost_estimate=pl.CostEstimate(
            flops=2 * rows * count * virtuals * atoms,
            bytes_accessed=2 * rows * count * (virtuals + atoms),
            transcendentals=0,
        ),
        name="back",
    )(slabs, coeffs)


def on_device(factors, occ_energy, vir_energy, coeffs):
    mine = factors[0]
    count = lax.axis_size(OCC)
    index = lax.axis_index(OCC)
    sign = 1 - 2 * (index % 2)
    places = jnp.stack([(index + sign * k) % count for k in range(-3, 4)])
    levels = (places, occ_energy, vir_energy[:, None], vir_energy[None, :])
    f32, bf16 = jnp.float32, jnp.bfloat16

    plus2 = mirrored(mine, count, -2)
    upper, lower, again = split(mine)
    minus2 = mirrored(again, count, 2)
    upper, lower = mirrored(upper, count, 1), mirrored(lower, count, 1)
    total, plus1 = first_pair(levels, (0, 1), mine, upper, lower)
    minus3 = mirrored(plus2, count, -1)
    total, beside = pairs_sum(
        levels, [mine, plus1, plus2], [((0, 2), 0, 2), ((1, 2), 1, 2)], [total], [f32, f32]
    )
    (beside,) = pairs_sum(levels, [plus1, minus2], [((1, -2), 0, 1)], [beside], [bf16])
    (total,) = pairs_sum(levels, [mine, minus2], [((0, -2), 0, 1)], [total], [f32])
    arrived = mirrored(beside, count, 1)
    gamma = last_pair(levels, (0, -3), mine, minus3, total, arrived)
    slabs = lax.all_to_all(gamma.reshape(count, -1, LANES), OCC, 0, 0, tiled=True)
    return back_transform(slabs.reshape(-1, LANES), coeffs, count)


def solution(mesh):
    finer = Mesh(
        mesh.devices.reshape(2, 4, 8, 2, mesh.shape["frag"]),
        ("occ_0", "occ_1", "occ_2", "occ_3", "frag"),
    )
    in_specs = (P(FRAG_OCC, None, None), P("frag"), P("frag"), P("frag", None))
    out_specs = P(OCC, "frag", None)
    return jax.shard_map(
        on_device, mesh=finer, in_specs=in_specs, out_specs=out_specs, check_vma=False
    )
```

```python
import functools

import jax
import jax.numpy as jnp
from jax import lax
from jax.experimental import pallas as pl
from jax.experimental.pallas import tpu as pltpu
from jax.sharding import Mesh
from jax.sharding import PartitionSpec as P

OCC = ("occ_0", "occ_1", "occ_2", "occ_3")
FRAG_OCC = ("frag",) + OCC
LANES = 128
PARTS = 2
VMEM_LIMIT = 40 * 1024 * 1024

NT = (((1,), (1,)), ((), ()))
TN = (((0,), (0,)), ((), ()))


def mirrored(block, count, step):
    route = [(i, (i + step if i % 2 == 0 else i - step) % count) for i in range(count)]
    return lax.ppermute(block, OCC, route)


def amplitudes(steps, levels, left, right):
    places, occ_energy, column, row = levels
    energy = occ_energy[places[steps[0] + 3]] + occ_energy[places[steps[1] + 3]]
    kmat = lax.dot_general(right[...], left[...], NT, preferred_element_type=jnp.float32)
    return (kmat / (energy - column[...] - row[...])).astype(jnp.bfloat16)


def pair_terms(amps, right):
    aux = right.shape[1]
    for start in range(0, aux, aux // PARTS):
        block = right[:, start : start + aux // PARTS]
        yield (
            pl.ds(start, aux // PARTS),
            lax.dot_general(block, amps, TN, preferred_element_type=jnp.float32),
        )


def pairs_kernel(pairs, blocks, carried, *refs):
    levels, refs = refs[:4], refs[4:]
    held, refs = refs[:blocks], refs[blocks:]
    totals, outs = refs[:carried], refs[carried:]
    for k, (steps, left, right) in enumerate(pairs):
        amps = amplitudes(steps, levels, held[left], held[right])
        for part, value in pair_terms(amps, held[right]):
            if k < carried:
                value = value + totals[k][part, :]
            outs[k][part, :] = value.astype(outs[k].dtype)


def first_kernel(steps, *refs):
    levels = refs[:4]
    mine, upper, lower, total, other = refs[4:]
    half = upper.shape[0]
    other[:half, :] = upper[...]
    other[half:, :] = lower[...]
    amps = amplitudes(steps, levels, mine, other)
    for part, value in pair_terms(amps, other):
        total[part, :] = value


def split_kernel(mine, upper, lower):
    half = upper.shape[0]
    upper[...] = mine[:half, :]
    lower[...] = mine[half:, :]


def split(mine):
    rows, aux = mine.shape
    vmem = pl.BlockSpec(memory_space=pltpu.VMEM)
    return pl.pallas_call(
        split_kernel,
        out_shape=[jax.ShapeDtypeStruct((rows // 2, aux), mine.dtype)] * 2,
        in_specs=[vmem],
        out_specs=[vmem] * 2,
        compiler_params=pltpu.CompilerParams(vmem_limit_bytes=VMEM_LIMIT),
        cost_estimate=pl.CostEstimate(flops=1000, bytes_accessed=1000, transcendentals=0),
        name="split",
    )(mine)


def amps_kernel(steps, *refs):
    levels = refs[:4]
    mine, other, out = refs[4:]
    out[...] = amplitudes(steps, levels, mine, other)


def last_kernel(amps, other, total, arrived, out, wide):
    cols = other.shape[0] // LANES
    for part, value in pair_terms(amps[...], other):
        value = value + total[part, :] + arrived[part, :].astype(jnp.float32)
        for c in range(cols):
            rows = pl.ds(part.start * cols + c, part.size, stride=cols)
            wide[rows, :] = value[:, c * LANES : (c + 1) * LANES]
    out[...] = wide[...].astype(out.dtype)


def local_call(kernel, levels, arrays, outs, scratch=(), name=None, flops=1000):
    vmem = pl.BlockSpec(memory_space=pltpu.VMEM)
    smem = pl.BlockSpec(memory_space=pltpu.SMEM)
    return pl.pallas_call(
        kernel,
        out_shape=[jax.ShapeDtypeStruct(shape, dtype) for shape, dtype in outs],
        in_specs=[smem] * 2 + [vmem] * (2 + len(arrays)),
        out_specs=[vmem] * len(outs),
        scratch_shapes=list(scratch),
        compiler_params=pltpu.CompilerParams(vmem_limit_bytes=VMEM_LIMIT),
        cost_estimate=pl.CostEstimate(flops=flops, bytes_accessed=1000, transcendentals=0),
        name=name,
    )(*levels, *arrays)


def pairs_sum(levels, blocks, pairs, totals, dtypes):
    shape = blocks[0].shape[::-1]
    kernel = functools.partial(pairs_kernel, pairs, len(blocks), len(totals))
    outs = [(shape, dtype) for dtype in dtypes]
    flops = 10**10 if len(pairs) > 1 else 1000
    return local_call(kernel, levels, [*blocks, *totals], outs, name="pairs", flops=flops)


def first_pair(levels, steps, mine, upper, lower):
    outs = [(mine.shape[::-1], jnp.float32), (mine.shape, mine.dtype)]
    kernel = functools.partial(first_kernel, steps)
    return local_call(kernel, levels, [mine, upper, lower], outs, name="first")


def last_pair(levels, steps, mine, other, total, arrived):
    virtuals, aux = mine.shape
    kernel = functools.partial(amps_kernel, steps)
    outs = [((virtuals, virtuals), jnp.bfloat16)]
    (amps,) = local_call(kernel, levels, [mine, other], outs, name="amps")
    shape = (mine.size // LANES, LANES)
    vmem = pl.BlockSpec(memory_space=pltpu.VMEM)
    return pl.pallas_call(
        last_kernel,
        out_shape=jax.ShapeDtypeStruct(shape, jnp.bfloat16),
        in_specs=[vmem] * 4,
        out_specs=vmem,
        scratch_shapes=[pltpu.VMEM(shape, jnp.float32)],
        compiler_params=pltpu.CompilerParams(vmem_limit_bytes=VMEM_LIMIT),
        cost_estimate=pl.CostEstimate(flops=1000, bytes_accessed=1000, transcendentals=0),
        name="last",
    )(amps, other, total, arrived)


def back_kernel(chunk, slabs, coeffs, out, wide, flat, done, sems):
    rows, count, _ = done.shape
    cols = coeffs.shape[1] // LANES
    wide[...] = slabs[...].astype(jnp.float32)
    copies = []
    for k in range(rows // chunk):
        for p in range(chunk):
            for c in range(cols):
                source = pl.ds(((k * chunk + p) * cols) + c, count, stride=rows * cols)
                flat[p * count : (p + 1) * count, c * LANES : (c + 1) * LANES] = wide[
                    source, :
                ].astype(flat.dtype)
        back = lax.dot_general(flat[...], coeffs[...], NT, preferred_element_type=jnp.float32)
        part = pl.ds(k * chunk, chunk)
        done[part] = back.astype(done.dtype).reshape(chunk, count, -1)
        copies.append(pltpu.make_async_copy(done.at[part], out.at[part], sems.at[k]))
        copies[-1].start()
    for copy in copies:
        copy.wait()


def back_transform(slabs, coeffs, count):
    atoms, virtuals = coeffs.shape
    rows = slabs.size // (count * virtuals)
    chunk = 2
    shape = (rows, count, atoms)
    vmem = pl.BlockSpec(memory_space=pltpu.VMEM)
    return pl.pallas_call(
        functools.partial(back_kernel, chunk),
        out_shape=jax.ShapeDtypeStruct(shape, jnp.bfloat16),
        in_specs=[vmem, vmem],
        out_specs=pl.BlockSpec(memory_space=pl.ANY),
        scratch_shapes=[
            pltpu.VMEM(slabs.shape, jnp.float32),
            pltpu.VMEM((chunk * count, virtuals), jnp.bfloat16),
            pltpu.VMEM(shape, jnp.bfloat16),
            pltpu.SemaphoreType.DMA((rows // chunk,)),
        ],
        compiler_params=pltpu.CompilerParams(vmem_limit_bytes=VMEM_LIMIT),
        cost_estimate=pl.CostEstimate(
            flops=2 * rows * count * virtuals * atoms,
            bytes_accessed=2 * rows * count * (virtuals + atoms),
            transcendentals=0,
        ),
        name="back",
    )(slabs, coeffs)


def on_device(factors, occ_energy, vir_energy, coeffs):
    mine = factors[0]
    count = lax.axis_size(OCC)
    index = lax.axis_index(OCC)
    sign = 1 - 2 * (index % 2)
    places = jnp.stack([(index + sign * k) % count for k in range(-3, 4)])
    levels = (places, occ_energy, vir_energy[:, None], vir_energy[None, :])
    f32, bf16 = jnp.float32, jnp.bfloat16

    plus2 = mirrored(mine, count, -2)
    upper, lower = split(mine)
    upper, lower = mirrored(upper, count, 1), mirrored(lower, count, 1)
    total, plus1 = first_pair(levels, (0, 1), mine, upper, lower)
    minus2 = mirrored(plus1, count, -1)
    minus3 = mirrored(plus2, count, -1)
    total, beside = pairs_sum(
        levels, [mine, plus1, plus2], [((0, 2), 0, 2), ((1, 2), 1, 2)], [total], [f32, f32]
    )
    (beside,) = pairs_sum(levels, [plus1, minus2], [((1, -2), 0, 1)], [beside], [bf16])
    (total,) = pairs_sum(levels, [mine, minus2], [((0, -2), 0, 1)], [total], [f32])
    arrived = mirrored(beside, count, 1)
    gamma = last_pair(levels, (0, -3), mine, minus3, total, arrived)
    slabs = lax.all_to_all(gamma.reshape(count, -1, LANES), OCC, 0, 0, tiled=True)
    return back_transform(slabs.reshape(-1, LANES), coeffs, count)


def solution(mesh):
    finer = Mesh(
        mesh.devices.reshape(2, 4, 8, 2, mesh.shape["frag"]),
        ("occ_0", "occ_1", "occ_2", "occ_3", "frag"),
    )
    in_specs = (P(FRAG_OCC, None, None), P("frag"), P("frag"), P("frag", None))
    out_specs = P(OCC, "frag", None)
    return jax.shard_map(
        on_device, mesh=finer, in_specs=in_specs, out_specs=out_specs, check_vma=False
    )
```

```python
import functools

import jax
import jax.numpy as jnp
from jax import lax
from jax.experimental import pallas as pl
from jax.experimental.pallas import tpu as pltpu
from jax.sharding import Mesh
from jax.sharding import PartitionSpec as P

OCC = ("occ_0", "occ_1", "occ_2", "occ_3")
FRAG_OCC = ("frag",) + OCC
LANES = 128
PARTS = 2
VMEM_LIMIT = 40 * 1024 * 1024

NT = (((1,), (1,)), ((), ()))
TN = (((0,), (0,)), ((), ()))


def mirrored(block, count, step):
    route = [(i, (i + step if i % 2 == 0 else i - step) % count) for i in range(count)]
    return lax.ppermute(block, OCC, route)


def amplitudes(steps, levels, left, right):
    places, occ_energy, column, row = levels
    energy = occ_energy[places[steps[0] + 3]] + occ_energy[places[steps[1] + 3]]
    kmat = lax.dot_general(right[...], left[...], NT, preferred_element_type=jnp.float32)
    return (kmat / (energy - column[...] - row[...])).astype(jnp.bfloat16)


def pair_terms(amps, right):
    aux = right.shape[1]
    for start in range(0, aux, aux // PARTS):
        block = right[:, start : start + aux // PARTS]
        yield (
            pl.ds(start, aux // PARTS),
            lax.dot_general(block, amps, TN, preferred_element_type=jnp.float32),
        )


def pairs_kernel(pairs, blocks, carried, *refs):
    levels, refs = refs[:4], refs[4:]
    held, refs = refs[:blocks], refs[blocks:]
    totals, outs = refs[:carried], refs[carried:]
    for k, (steps, left, right) in enumerate(pairs):
        amps = amplitudes(steps, levels, held[left], held[right])
        for part, value in pair_terms(amps, held[right]):
            if k < carried:
                value = value + totals[k][part, :]
            outs[k][part, :] = value.astype(outs[k].dtype)


def joined_kernel(steps, carried, *refs):
    levels = refs[:4]
    left, upper, lower, *totals, out, other = refs[4:]
    half = upper.shape[0]
    other[:half, :] = upper[...]
    other[half:, :] = lower[...]
    amps = amplitudes(steps, levels, left, other)
    for part, value in pair_terms(amps, other):
        if carried:
            value = value + totals[0][part, :]
        out[part, :] = value.astype(out.dtype)


def split_kernel(mine, upper, lower):
    half = upper.shape[0]
    upper[...] = mine[:half, :]
    lower[...] = mine[half:, :]


def split(mine):
    rows, aux = mine.shape
    vmem = pl.BlockSpec(memory_space=pltpu.VMEM)
    return pl.pallas_call(
        split_kernel,
        out_shape=[jax.ShapeDtypeStruct((rows // 2, aux), mine.dtype)] * 2,
        in_specs=[vmem],
        out_specs=[vmem] * 2,
        compiler_params=pltpu.CompilerParams(vmem_limit_bytes=VMEM_LIMIT),
        cost_estimate=pl.CostEstimate(flops=1000, bytes_accessed=1000, transcendentals=0),
        name="split",
    )(mine)


def amps_kernel(steps, *refs):
    levels = refs[:4]
    mine, other, out = refs[4:]
    out[...] = amplitudes(steps, levels, mine, other)


def last_kernel(amps, other, total, arrived, out, wide):
    cols = other.shape[0] // LANES
    for part, value in pair_terms(amps[...], other):
        value = value + total[part, :] + arrived[part, :].astype(jnp.float32)
        for c in range(cols):
            rows = pl.ds(part.start * cols + c, part.size, stride=cols)
            wide[rows, :] = value[:, c * LANES : (c + 1) * LANES]
    out[...] = wide[...].astype(out.dtype)


def local_call(kernel, levels, arrays, outs, scratch=(), name=None):
    vmem = pl.BlockSpec(memory_space=pltpu.VMEM)
    smem = pl.BlockSpec(memory_space=pltpu.SMEM)
    return pl.pallas_call(
        kernel,
        out_shape=[jax.ShapeDtypeStruct(shape, dtype) for shape, dtype in outs],
        in_specs=[smem] * 2 + [vmem] * (2 + len(arrays)),
        out_specs=[vmem] * len(outs),
        scratch_shapes=list(scratch),
        compiler_params=pltpu.CompilerParams(vmem_limit_bytes=VMEM_LIMIT),
        cost_estimate=pl.CostEstimate(flops=1000, bytes_accessed=1000, transcendentals=0),
        name=name,
    )(*levels, *arrays)


def pairs_sum(levels, blocks, pairs, totals, dtypes):
    shape = blocks[0].shape[::-1]
    kernel = functools.partial(pairs_kernel, pairs, len(blocks), len(totals))
    outs = [(shape, dtype) for dtype in dtypes]
    return local_call(kernel, levels, [*blocks, *totals], outs, name="pairs")


def joined_pair(levels, steps, left, halves, totals, dtype, name):
    outs = [(left.shape[::-1], dtype), (left.shape, left.dtype)]
    kernel = functools.partial(joined_kernel, steps, len(totals))
    return local_call(kernel, levels, [left, *halves, *totals], outs, name=name)


def last_pair(levels, steps, mine, other, total, arrived):
    virtuals, aux = mine.shape
    kernel = functools.partial(amps_kernel, steps)
    outs = [((virtuals, virtuals), jnp.bfloat16)]
    (amps,) = local_call(kernel, levels, [mine, other], outs, name="amps")
    shape = (mine.size // LANES, LANES)
    vmem = pl.BlockSpec(memory_space=pltpu.VMEM)
    return pl.pallas_call(
        last_kernel,
        out_shape=jax.ShapeDtypeStruct(shape, jnp.bfloat16),
        in_specs=[vmem] * 4,
        out_specs=vmem,
        scratch_shapes=[pltpu.VMEM(shape, jnp.float32)],
        compiler_params=pltpu.CompilerParams(vmem_limit_bytes=VMEM_LIMIT),
        cost_estimate=pl.CostEstimate(flops=1000, bytes_accessed=1000, transcendentals=0),
        name="last",
    )(amps, other, total, arrived)


def back_kernel(chunk, slabs, coeffs, out, wide, flat, done, sems):
    rows, count, _ = done.shape
    cols = coeffs.shape[1] // LANES
    wide[...] = slabs[...].astype(jnp.float32)
    copies = []
    for k in range(rows // chunk):
        for p in range(chunk):
            for c in range(cols):
                source = pl.ds(((k * chunk + p) * cols) + c, count, stride=rows * cols)
                flat[p * count : (p + 1) * count, c * LANES : (c + 1) * LANES] = wide[
                    source, :
                ].astype(flat.dtype)
        back = lax.dot_general(flat[...], coeffs[...], NT, preferred_element_type=jnp.float32)
        part = pl.ds(k * chunk, chunk)
        done[part] = back.astype(done.dtype).reshape(chunk, count, -1)
        copies.append(pltpu.make_async_copy(done.at[part], out.at[part], sems.at[k]))
        copies[-1].start()
    for copy in copies:
        copy.wait()


def back_transform(slabs, coeffs, count):
    atoms, virtuals = coeffs.shape
    rows = slabs.size // (count * virtuals)
    chunk = 2
    shape = (rows, count, atoms)
    vmem = pl.BlockSpec(memory_space=pltpu.VMEM)
    return pl.pallas_call(
        functools.partial(back_kernel, chunk),
        out_shape=jax.ShapeDtypeStruct(shape, jnp.bfloat16),
        in_specs=[vmem, vmem],
        out_specs=pl.BlockSpec(memory_space=pl.ANY),
        scratch_shapes=[
            pltpu.VMEM(slabs.shape, jnp.float32),
            pltpu.VMEM((chunk * count, virtuals), jnp.bfloat16),
            pltpu.VMEM(shape, jnp.bfloat16),
            pltpu.SemaphoreType.DMA((rows // chunk,)),
        ],
        compiler_params=pltpu.CompilerParams(vmem_limit_bytes=VMEM_LIMIT),
        cost_estimate=pl.CostEstimate(
            flops=2 * rows * count * virtuals * atoms,
            bytes_accessed=2 * rows * count * (virtuals + atoms),
            transcendentals=0,
        ),
        name="back",
    )(slabs, coeffs)


def on_device(factors, occ_energy, vir_energy, coeffs):
    mine = factors[0]
    count = lax.axis_size(OCC)
    index = lax.axis_index(OCC)
    sign = 1 - 2 * (index % 2)
    places = jnp.stack([(index + sign * k) % count for k in range(-3, 4)])
    levels = (places, occ_energy, vir_energy[:, None], vir_energy[None, :])
    f32, bf16 = jnp.float32, jnp.bfloat16

    plus2 = mirrored(mine, count, -2)
    halves = [mirrored(half, count, 1) for half in split(mine)]
    far_halves = [mirrored(half, count, -1) for half in halves]
    total, plus1 = joined_pair(levels, (0, 1), mine, halves, [], f32, "first")
    minus3 = mirrored(plus2, count, -1)
    total, beside = pairs_sum(
        levels, [mine, plus1, plus2], [((0, 2), 0, 2), ((1, 2), 1, 2)], [total], [f32, f32]
    )
    beside, minus2 = joined_pair(levels, (1, -2), plus1, far_halves, [beside], bf16, "beside")
    (total,) = pairs_sum(levels, [mine, minus2], [((0, -2), 0, 1)], [total], [f32])
    arrived = mirrored(beside, count, 1)
    gamma = last_pair(levels, (0, -3), mine, minus3, total, arrived)
    slabs = lax.all_to_all(gamma.reshape(count, -1, LANES), OCC, 0, 0, tiled=True)
    return back_transform(slabs.reshape(-1, LANES), coeffs, count)


def solution(mesh):
    finer = Mesh(
        mesh.devices.reshape(2, 4, 8, 2, mesh.shape["frag"]),
        ("occ_0", "occ_1", "occ_2", "occ_3", "frag"),
    )
    in_specs = (P(FRAG_OCC, None, None), P("frag"), P("frag"), P("frag", None))
    out_specs = P(OCC, "frag", None)
    return jax.shard_map(
        on_device, mesh=finer, in_specs=in_specs, out_specs=out_specs, check_vma=False
    )
```

```python
import functools

import jax
import jax.numpy as jnp
from jax import lax
from jax.experimental import pallas as pl
from jax.experimental.pallas import tpu as pltpu
from jax.sharding import Mesh
from jax.sharding import PartitionSpec as P

OCC = ("occ_0", "occ_1", "occ_2", "occ_3")
FRAG_OCC = ("frag",) + OCC
LANES = 128
PARTS = 2
VMEM_LIMIT = 40 * 1024 * 1024

NT = (((1,), (1,)), ((), ()))
TN = (((0,), (0,)), ((), ()))


def mirrored(block, count, step):
    route = [(i, (i + step if i % 2 == 0 else i - step) % count) for i in range(count)]
    return lax.ppermute(block, OCC, route)


def amplitudes(steps, levels, left, right):
    places, occ_energy, column, row = levels
    energy = occ_energy[places[steps[0] + 3]] + occ_energy[places[steps[1] + 3]]
    kmat = lax.dot_general(right[...], left[...], NT, preferred_element_type=jnp.float32)
    return (kmat / (energy - column[...] - row[...])).astype(jnp.bfloat16)


def pair_terms(amps, right):
    aux = right.shape[1]
    for start in range(0, aux, aux // PARTS):
        block = right[:, start : start + aux // PARTS]
        yield (
            pl.ds(start, aux // PARTS),
            lax.dot_general(block, amps, TN, preferred_element_type=jnp.float32),
        )


def pairs_kernel(pairs, blocks, carried, *refs):
    levels, refs = refs[:4], refs[4:]
    held, refs = refs[:blocks], refs[blocks:]
    totals, outs = refs[:carried], refs[carried:]
    for k, (steps, left, right) in enumerate(pairs):
        amps = amplitudes(steps, levels, held[left], held[right])
        for part, value in pair_terms(amps, held[right]):
            if k < carried:
                value = value + totals[k][part, :]
            outs[k][part, :] = value.astype(outs[k].dtype)


def joined_kernel(steps, carried, *refs):
    levels = refs[:4]
    left, upper, lower, *totals, out, other = refs[4:]
    half = upper.shape[0]
    other[:half, :] = upper[...]
    other[half:, :] = lower[...]
    amps = amplitudes(steps, levels, left, other)
    for part, value in pair_terms(amps, other):
        if carried:
            value = value + totals[0][part, :]
        out[part, :] = value.astype(out.dtype)


def near_kernel(*refs):
    levels = refs[:4]
    mine, upper, lower, plus2, total, beside, plus1 = refs[4:]
    half = upper.shape[0]
    plus1[:half, :] = upper[...]
    plus1[half:, :] = lower[...]
    amps = amplitudes((0, 1), levels, mine, plus1)
    for part, value in pair_terms(amps, plus1):
        total[part, :] = value
    amps = amplitudes((0, 2), levels, mine, plus2)
    for part, value in pair_terms(amps, plus2):
        total[part, :] = total[part, :] + value
    amps = amplitudes((1, 2), levels, plus1, plus2)
    for part, value in pair_terms(amps, plus2):
        beside[part, :] = value


def split_kernel(mine, upper, lower):
    half = upper.shape[0]
    upper[...] = mine[:half, :]
    lower[...] = mine[half:, :]


def split(mine):
    rows, aux = mine.shape
    vmem = pl.BlockSpec(memory_space=pltpu.VMEM)
    return pl.pallas_call(
        split_kernel,
        out_shape=[jax.ShapeDtypeStruct((rows // 2, aux), mine.dtype)] * 2,
        in_specs=[vmem],
        out_specs=[vmem] * 2,
        compiler_params=pltpu.CompilerParams(vmem_limit_bytes=VMEM_LIMIT),
        cost_estimate=pl.CostEstimate(flops=1000, bytes_accessed=1000, transcendentals=0),
        name="split",
    )(mine)


def amps_kernel(steps, *refs):
    levels = refs[:4]
    mine, other, out = refs[4:]
    out[...] = amplitudes(steps, levels, mine, other)


def last_kernel(amps, other, total, arrived, out, wide):
    cols = other.shape[0] // LANES
    for part, value in pair_terms(amps[...], other):
        value = value + total[part, :] + arrived[part, :].astype(jnp.float32)
        for c in range(cols):
            rows = pl.ds(part.start * cols + c, part.size, stride=cols)
            wide[rows, :] = value[:, c * LANES : (c + 1) * LANES]
    out[...] = wide[...].astype(out.dtype)


def local_call(kernel, levels, arrays, outs, scratch=(), name=None):
    vmem = pl.BlockSpec(memory_space=pltpu.VMEM)
    smem = pl.BlockSpec(memory_space=pltpu.SMEM)
    return pl.pallas_call(
        kernel,
        out_shape=[jax.ShapeDtypeStruct(shape, dtype) for shape, dtype in outs],
        in_specs=[smem] * 2 + [vmem] * (2 + len(arrays)),
        out_specs=[vmem] * len(outs),
        scratch_shapes=list(scratch),
        compiler_params=pltpu.CompilerParams(vmem_limit_bytes=VMEM_LIMIT),
        cost_estimate=pl.CostEstimate(flops=1000, bytes_accessed=1000, transcendentals=0),
        name=name,
    )(*levels, *arrays)


def pairs_sum(levels, blocks, pairs, totals, dtypes):
    shape = blocks[0].shape[::-1]
    kernel = functools.partial(pairs_kernel, pairs, len(blocks), len(totals))
    outs = [(shape, dtype) for dtype in dtypes]
    return local_call(kernel, levels, [*blocks, *totals], outs, name="pairs")


def joined_pair(levels, steps, left, halves, totals, dtype, name):
    outs = [(left.shape[::-1], dtype), (left.shape, left.dtype)]
    kernel = functools.partial(joined_kernel, steps, len(totals))
    return local_call(kernel, levels, [left, *halves, *totals], outs, name=name)


def last_pair(levels, steps, mine, other, total, arrived):
    virtuals, aux = mine.shape
    kernel = functools.partial(amps_kernel, steps)
    outs = [((virtuals, virtuals), jnp.bfloat16)]
    (amps,) = local_call(kernel, levels, [mine, other], outs, name="amps")
    shape = (mine.size // LANES, LANES)
    vmem = pl.BlockSpec(memory_space=pltpu.VMEM)
    return pl.pallas_call(
        last_kernel,
        out_shape=jax.ShapeDtypeStruct(shape, jnp.bfloat16),
        in_specs=[vmem] * 4,
        out_specs=vmem,
        scratch_shapes=[pltpu.VMEM(shape, jnp.float32)],
        compiler_params=pltpu.CompilerParams(vmem_limit_bytes=VMEM_LIMIT),
        cost_estimate=pl.CostEstimate(flops=1000, bytes_accessed=1000, transcendentals=0),
        name="last",
    )(amps, other, total, arrived)


def back_kernel(chunk, slabs, coeffs, out, wide, flat, done, sems):
    rows, count, _ = done.shape
    cols = coeffs.shape[1] // LANES
    wide[...] = slabs[...].astype(jnp.float32)
    copies = []
    for k in range(rows // chunk):
        for p in range(chunk):
            for c in range(cols):
                source = pl.ds(((k * chunk + p) * cols) + c, count, stride=rows * cols)
                flat[p * count : (p + 1) * count, c * LANES : (c + 1) * LANES] = wide[
                    source, :
                ].astype(flat.dtype)
        back = lax.dot_general(flat[...], coeffs[...], NT, preferred_element_type=jnp.float32)
        part = pl.ds(k * chunk, chunk)
        done[part] = back.astype(done.dtype).reshape(chunk, count, -1)
        copies.append(pltpu.make_async_copy(done.at[part], out.at[part], sems.at[k]))
        copies[-1].start()
    for copy in copies:
        copy.wait()


def back_transform(slabs, coeffs, count):
    atoms, virtuals = coeffs.shape
    rows = slabs.size // (count * virtuals)
    chunk = 2
    shape = (rows, count, atoms)
    vmem = pl.BlockSpec(memory_space=pltpu.VMEM)
    return pl.pallas_call(
        functools.partial(back_kernel, chunk),
        out_shape=jax.ShapeDtypeStruct(shape, jnp.bfloat16),
        in_specs=[vmem, vmem],
        out_specs=pl.BlockSpec(memory_space=pl.ANY),
        scratch_shapes=[
            pltpu.VMEM(slabs.shape, jnp.float32),
            pltpu.VMEM((chunk * count, virtuals), jnp.bfloat16),
            pltpu.VMEM(shape, jnp.bfloat16),
            pltpu.SemaphoreType.DMA((rows // chunk,)),
        ],
        compiler_params=pltpu.CompilerParams(vmem_limit_bytes=VMEM_LIMIT),
        cost_estimate=pl.CostEstimate(
            flops=2 * rows * count * virtuals * atoms,
            bytes_accessed=2 * rows * count * (virtuals + atoms),
            transcendentals=0,
        ),
        name="back",
    )(slabs, coeffs)


def on_device(factors, occ_energy, vir_energy, coeffs):
    mine = factors[0]
    count = lax.axis_size(OCC)
    index = lax.axis_index(OCC)
    sign = 1 - 2 * (index % 2)
    places = jnp.stack([(index + sign * k) % count for k in range(-3, 4)])
    levels = (places, occ_energy, vir_energy[:, None], vir_energy[None, :])
    f32, bf16 = jnp.float32, jnp.bfloat16

    plus2 = mirrored(mine, count, -2)
    halves = [mirrored(half, count, 1) for half in split(mine)]
    far_halves = [mirrored(half, count, -1) for half in halves]
    minus3 = mirrored(plus2, count, -1)
    shape = (mine.shape[::-1], f32)
    outs = [shape, shape, (mine.shape, mine.dtype)]
    total, beside, plus1 = local_call(
        near_kernel, levels, [mine, *halves, plus2], outs, name="first"
    )
    beside, minus2 = joined_pair(levels, (1, -2), plus1, far_halves, [beside], bf16, "beside")
    (total,) = pairs_sum(levels, [mine, minus2], [((0, -2), 0, 1)], [total], [f32])
    arrived = mirrored(beside, count, 1)
    gamma = last_pair(levels, (0, -3), mine, minus3, total, arrived)
    slabs = lax.all_to_all(gamma.reshape(count, -1, LANES), OCC, 0, 0, tiled=True)
    return back_transform(slabs.reshape(-1, LANES), coeffs, count)


def solution(mesh):
    finer = Mesh(
        mesh.devices.reshape(2, 4, 8, 2, mesh.shape["frag"]),
        ("occ_0", "occ_1", "occ_2", "occ_3", "frag"),
    )
    in_specs = (P(FRAG_OCC, None, None), P("frag"), P("frag"), P("frag", None))
    out_specs = P(OCC, "frag", None)
    return jax.shard_map(
        on_device, mesh=finer, in_specs=in_specs, out_specs=out_specs, check_vma=False
    )
```
